32 devices in a mesh: layer: 8 (over y, x, core), feat: 4 (over z).
Axes of the slice: x: 2, y: 2, z: 4, core: 2. Of those that a mesh axis runs over, the one named last changes fastest.
Arguments:
- pre_acts: bfloat16 [8, 512, 512], P('layer', None, 'feat'), may hold values from -6 to 6
- decoder: bfloat16 [8, 8, 512, 2048], P('layer', None, 'feat'), may hold values from -0.125 to 0.125
- dec_bias: bfloat16 [8, 2048], P('layer', 'feat'), may hold values from -3 to 3
- target: bfloat16 [8, 512, 2048], P('layer', None, 'feat'), may hold values from -6 to 6
Outputs:
- recon_error: float32 [8, 512, 2048], P('layer', None, 'feat')
- pre_grad: float32 [8, 512, 512], P('layer', None, 'feat')
The draws below stay inside these ranges and needn't reach their ends.
All inputs are finite; a program needn't handle non-finite values.
Results may differ from the reference program's by a relative error of at most 0.015.
Values may be sent and summed in bfloat16 or wider, within the bound.
A program may use at most 64 MiB of HBM per device.

```python
import jax
import jax.numpy as jnp
from jax import lax

D = 2048
FEAT_DEV = 128
TOKENS = 512
LAYERS = 8
FEATURES = 512
N_FEAT = 4


def shard_levels(rng, dims, split, smallest, high):
    loudness, own = 1.0, jax.random.fold_in(rng, 6)
    for dim, parts in split:
        heights = jnp.exp(jax.random.uniform(jax.random.fold_in(own, dim), (parts,), jnp.float32, smallest / len(split), high / len(split)))
        loudness = loudness * jnp.repeat(heights, dims[dim] // parts).reshape([-1 if axis == dim else 1 for axis in range(len(dims))])
    return loudness


def noise(key, shape, scale, limit, split=(), kind=jnp.bfloat16):
    entries = jax.random.normal(key, shape, jnp.float32) * scale
    if len(split) > 0:
        entries = shard_levels(key, shape, split, -0.22, 0.18) * entries
    return jnp.clip(entries, min=-limit, max=limit).astype(kind)


def setup_inputs(seed: int = 0) -> dict:
    seeds = jax.random.split(jax.random.key(seed), 5)
    pre_acts = noise(seeds[0], (LAYERS, TOKENS, FEATURES), 1.0, 6.0, ((0, 8), (2, 4)))
    decoder = noise(seeds[1], (LAYERS, LAYERS, FEATURES, D), (FEATURES * LAYERS // 2) ** -0.5, 0.125, ((0, 8), (2, 4)))
    dec_bias = noise(seeds[2], (LAYERS, D), 0.5, 3.0, ((0, 8), (1, 4)))
    target = noise(seeds[3], (LAYERS, TOKENS, D), 1.0, 6.0, ((0, 8), (2, 4)))
    return {"pre_acts": pre_acts, "decoder": decoder, "dec_bias": dec_bias, "target": target}


def rounded(value):
    return lax.optimization_barrier(value.astype(jnp.bfloat16)).astype(jnp.float32)


def reference(pre_acts, decoder, dec_bias, target):
    token_count = pre_acts.shape[1]
    activations = jnp.maximum(pre_acts, jnp.zeros((), pre_acts.dtype)).astype(jnp.float32)
    blocked = activations.reshape(LAYERS, token_count, N_FEAT, FEAT_DEV)
    errors = []
    for target_layer in range(LAYERS):
        partial_value = jnp.zeros((N_FEAT, token_count, D), jnp.float32)
        for source_layer in range(target_layer + 1):
            weights = decoder[target_layer, source_layer].astype(jnp.float32).reshape(N_FEAT, FEAT_DEV, D)
            partial_value = partial_value + jnp.einsum("nbf,bfd->bnd", blocked[source_layer], weights)
        summed = jnp.sum(rounded(partial_value), axis=0)
        errors.append(summed + dec_bias[target_layer].astype(jnp.float32)[None, :] - target[target_layer].astype(jnp.float32))
    recon_error = jnp.stack(errors)
    error_rounded = rounded(recon_error)
    grads = []
    for source_layer in range(LAYERS):
        running = jnp.zeros((token_count, FEATURES), jnp.float32)
        for target_layer in range(source_layer, LAYERS):
            weights = decoder[target_layer, source_layer].astype(jnp.float32)
            product = jnp.einsum("nd,fd->nf", error_rounded[target_layer], weights)
            running = running + rounded(product)
        grads.append(running * (pre_acts[source_layer] > 0).astype(jnp.float32))
    return recon_error, jnp.stack(grads)
```

```python
import functools

import jax
import jax.numpy as jnp
from jax import lax
from jax.experimental import pallas as pl
from jax.experimental.pallas import tpu as pltpu
from jax.sharding import PartitionSpec as P

MESH = pl.DeviceIdType.MESH
F32 = jnp.float32
BF16 = jnp.bfloat16


def kernel(
    n_layer, n_feat, n_step, n_block, lag_outer,
    pre_ref, dec_ref, bias_ref, tgt_ref,
    err_ref, grad_ref,
    acts, weights, own, arrived, sent, half_in, error, terms, terms_in, tgt,
    w_sem, t_sem, out_sem,
    act_send, act_recv, p_send, p_recv, h_send, h_recv,
    e_in_send, e_out_send, e_recv, f_send, f_recv, term_send, term_recv,
):
    layer, feat = lax.axis_index("layer"), lax.axis_index("feat")
    tokens, width = pre_ref.shape
    model = weights.shape[1]
    shard = tgt.shape[1]
    half = model // 2
    rows_step, rows_block = tokens // n_step, tokens // n_block
    per_block = n_step // n_block
    tile = 512 if model % 512 == 0 else model
    mid = n_feat // 2
    left = feat < mid
    inward = jnp.where(left, feat + 1, feat - 1)
    outward = jnp.where(left, feat - 1, feat + 1)
    has_outward = jnp.logical_and(feat > 0, feat < n_feat - 1)
    is_mid = jnp.logical_or(feat == mid - 1, feat == mid)
    not_mid = jnp.logical_not(is_mid)

    def layer_cols(index):
        return pl.ds(pl.multiple_of(index * width, width), width)

    near = pl.ds(pl.multiple_of(jnp.where(left, 0, half), half), half)
    far = pl.ds(pl.multiple_of(jnp.where(left, half, 0), half), half)
    own_cols = pl.ds(pl.multiple_of(feat * shard, shard), shard)

    def step_rows(i):
        return pl.ds(pl.multiple_of(i * rows_step, rows_step), rows_step)

    def block_rows(b):
        return pl.ds(pl.multiple_of(b * rows_block, rows_block), rows_block)

    def w_copy(s):
        rows = pl.ds(s * width, width)
        return pltpu.make_async_copy(dec_ref.at[rows, :], weights.at[rows, :], w_sem.at[s])

    for s in range(n_layer):
        w_copy(s).start()
    t_copy = pltpu.make_async_copy(tgt_ref, tgt, t_sem)
    t_copy.start()

    barrier = pltpu.get_barrier_semaphore()
    for t in range(n_layer):
        @pl.when(t != layer)
        def _():
            pl.semaphore_signal(barrier, inc=1, device_id=(t, feat), device_id_type=MESH)
    pl.semaphore_signal(barrier, inc=1, device_id=(layer, inward), device_id_type=MESH)

    @pl.when(has_outward)
    def _():
        pl.semaphore_signal(barrier, inc=1, device_id=(layer, outward), device_id_type=MESH)

    acts[:, layer_cols(layer)] = jnp.maximum(pre_ref[...], jnp.zeros((), BF16))
    for s in range(n_layer):
        @pl.when(s > layer)
        def _():
            acts[:, s * width:(s + 1) * width] = jnp.zeros((tokens, width), BF16)

    pl.semaphore_wait(barrier, n_layer + has_outward.astype(jnp.int32))

    def act_copy(t, b, s):
        rows = block_rows(b)
        view = acts.at[rows, layer_cols(s)]
        return pltpu.make_async_remote_copy(
            src_ref=view, dst_ref=view, send_sem=act_send.at[t, b], recv_sem=act_recv.at[s, b],
            device_id=(t, feat), device_id_type=MESH)

    for b in range(n_block):
        for t in reversed(range(1, n_layer)):
            @pl.when(t > layer)
            def _():
                act_copy(t, b, layer).start()

    for s in range(n_layer):
        w_copy(s).wait()
    t_copy.wait()

    def p_copy(i):
        rows = step_rows(i)
        return pltpu.make_async_remote_copy(
            src_ref=sent.at[rows, :], dst_ref=arrived.at[rows, :],
            send_sem=p_send.at[i], recv_sem=p_recv.at[i],
            device_id=(layer, inward), device_id_type=MESH)

    def h_copy(i):
        rows = step_rows(i)
        return pltpu.make_async_remote_copy(
            src_ref=sent.at[rows, far], dst_ref=half_in.at[rows, :],
            send_sem=h_send.at[i], recv_sem=h_recv.at[i],
            device_id=(layer, inward), device_id_type=MESH)

    def e_copy(i, cols, send, recv, to):
        rows = step_rows(i)
        view = error.at[rows, cols]
        return pltpu.make_async_remote_copy(
            src_ref=view, dst_ref=view, send_sem=send.at[i], recv_sem=recv.at[i],
            device_id=(layer, to), device_id_type=MESH)

    def out_copy(i):
        rows = step_rows(i)
        return pltpu.make_async_copy(error.at[rows, own_cols], err_ref.at[rows, :], out_sem.at[i])

    def forward(b):
        rows = block_rows(b)
        for s in range(n_layer - 1):
            @pl.when(s < layer)
            def _():
                act_copy(layer, b, s).wait_recv()

        def one(c, _):
            cols = pl.ds(pl.multiple_of(c * tile, tile), tile)
            own[rows, cols] = jnp.dot(acts[rows, :], weights[:, cols], preferred_element_type=F32)
            return 0

        lax.fori_loop(0, model // tile, one, 0)
        own[rows, own_cols] += bias_ref[...].astype(F32) - tgt[rows, :].astype(F32)

    def send_partial(i):
        rows = step_rows(i)

        @pl.when(has_outward)
        def _():
            p_copy(i).wait_recv()

            @pl.when(is_mid)
            def _():
                sent[rows, far] = (own[rows, far] + arrived[rows, far].astype(F32)).astype(BF16)
                h_copy(i).start()
                own[rows, near] += arrived[rows, near].astype(F32)

            @pl.when(not_mid)
            def _():
                sent[rows, :] = (own[rows, :] + arrived[rows, :].astype(F32)).astype(BF16)
                p_copy(i).start()

        @pl.when(jnp.logical_not(has_outward))
        def _():
            @pl.when(is_mid)
            def _():
                sent[rows, far] = own[rows, far].astype(BF16)
                h_copy(i).start()

            @pl.when(not_mid)
            def _():
                sent[rows, :] = own[rows, :].astype(BF16)
                p_copy(i).start()

    def finish_half(i):
        rows = step_rows(i)
        h_copy(i).wait_recv()
        error[rows, near] = (own[rows, near] + half_in[rows, :].astype(F32)).astype(BF16)
        e_copy(i, near, e_in_send, f_recv, inward).start()

        @pl.when(has_outward)
        def _():
            e_copy(i, near, e_out_send, e_recv, outward).start()

    def pass_error(i):
        @pl.when(not_mid)
        def _():
            e_copy(i, near, e_out_send, e_recv, inward).wait_recv()

            @pl.when(has_outward)
            def _():
                e_copy(i, near, e_out_send, e_recv, outward).start()

        e_copy(i, far, f_send, f_recv, inward).wait_recv()

        @pl.when(has_outward)
        def _():
            e_copy(i, far, f_send, f_recv, outward).start()

        out_copy(i).start()

    def term_copy(s, b, t):
        rows = block_rows(b)
        return pltpu.make_async_remote_copy(
            src_ref=terms.at[rows, layer_cols(s)], dst_ref=terms_in.at[t, rows, :],
            send_sem=term_send.at[s, b], recv_sem=term_recv.at[t, b],
            device_id=(s, feat), device_id_type=MESH)

    def backward(b):
        rows = block_rows(b)
        step = 2 * width

        def one(c, _):
            cols = pl.ds(pl.multiple_of(c * step, step), step)
            terms[rows, cols] = lax.dot_general(
                error[rows, :], weights[cols, :], (((1,), (1,)), ((), ())),
                preferred_element_type=F32).astype(BF16)
            return 0

        lax.fori_loop(0, n_layer // 2, one, 0)
        for s in range(n_layer - 1):
            @pl.when(s < layer)
            def _():
                term_copy(s, b, layer).start()

    def collect(b):
        rows = block_rows(b)
        grad_ref[rows, :] = terms[rows, layer_cols(layer)].astype(F32)
        for t in range(1, n_layer):
            @pl.when(t > layer)
            def _():
                term_copy(layer, b, t).wait_recv()
                grad_ref[rows, :] += terms_in[t, rows, :].astype(F32)

    lag = jnp.where(is_mid, 2, lag_outer)

    def body(i, _):
        @pl.when(jnp.logical_and(i < n_step, lax.rem(i, per_block) == 0))
        def _():
            forward(lax.div(i, per_block))

        @pl.when(i < n_step)
        def _():
            send_partial(i)

        @pl.when(jnp.logical_and(is_mid, jnp.logical_and(i >= 1, i <= n_step)))
        def _():
            finish_half(i - 1)

        j = i - lag

        @pl.when(jnp.logical_and(j >= 0, j < n_step))
        def _():
            pass_error(j)

        @pl.when(jnp.logical_and(j >= 0, jnp.logical_and(j < n_step, lax.rem(j, per_block) == per_block - 1)))
        def _():
            backward(lax.div(j, per_block))

        return 0

    lax.fori_loop(0, n_step + lag_outer, body, 0)

    def tail(b, _):
        collect(b)
        return 0

    lax.fori_loop(0, n_block, tail, 0)

    def drain(i, _):
        @pl.when(not_mid)
        def _():
            p_copy(i).wait_send()

        @pl.when(is_mid)
        def _():
            h_copy(i).wait_send()
            e_copy(i, near, e_in_send, f_recv, inward).wait_send()

        @pl.when(has_outward)
        def _():
            e_copy(i, near, e_out_send, e_recv, outward).wait_send()
            e_copy(i, far, f_send, f_recv, outward).wait_send()

        out_copy(i).wait()
        return 0

    lax.fori_loop(0, n_step, drain, 0)

    def drain_block(b, _):
        for t in range(1, n_layer):
            @pl.when(t > layer)
            def _():
                act_copy(t, b, layer).wait_send()
        for s in range(n_layer - 1):
            @pl.when(s < layer)
            def _():
                term_copy(s, b, layer).wait_send()
        return 0

    lax.fori_loop(0, n_block, drain_block, 0)


def on_device(n_layer, n_feat, pre_acts, decoder, dec_bias, target):
    _, tokens, width = pre_acts.shape
    model = decoder.shape[3]
    shard = target.shape[2]
    n_step, n_block = 16, 4
    any_space = pl.BlockSpec(memory_space=pl.ANY)
    vmem = pl.BlockSpec(memory_space=pltpu.VMEM)
    dma = pltpu.SemaphoreType.DMA
    flops = 4 * tokens * n_layer * width * model
    error, grad = pl.pallas_call(
        functools.partial(kernel, n_layer, n_feat, n_step, n_block, 6),
        out_shape=(
            jax.ShapeDtypeStruct((tokens, shard), BF16),
            jax.ShapeDtypeStruct((tokens, width), F32),
        ),
        in_specs=[vmem, any_space, vmem, any_space],
        out_specs=(any_space, vmem),
        scratch_shapes=[
            pltpu.VMEM((tokens, n_layer * width), BF16),
            pltpu.VMEM((n_layer * width, model), BF16),
            pltpu.VMEM((tokens, model), F32),
            pltpu.VMEM((tokens, model), BF16),
            pltpu.VMEM((tokens, model), BF16),
            pltpu.VMEM((tokens, model // 2), BF16),
            pltpu.VMEM((tokens, model), BF16),
            pltpu.VMEM((tokens, n_layer * width), BF16),
            pltpu.VMEM((n_layer, tokens, width), BF16),
            pltpu.VMEM((tokens, shard), BF16),
            dma((n_layer,)), dma, dma((n_step,)),
            dma((n_layer, n_block)), dma((n_layer, n_block)),
            dma((n_step,)), dma((n_step,)), dma((n_step,)), dma((n_step,)),
            dma((n_step,)), dma((n_step,)), dma((n_step,)), dma((n_step,)), dma((n_step,)),
            dma((n_layer, n_block)), dma((n_layer, n_block)),
        ],
        compiler_params=pltpu.CompilerParams(
            collective_id=0, has_side_effects=True, vmem_limit_bytes=50 * 1024 * 1024),
        cost_estimate=pl.CostEstimate(
            flops=flops, bytes_accessed=2 * n_layer * width * model, transcendentals=0),
    )(
        pre_acts[0],
        decoder.reshape(n_layer * width, model),
        dec_bias,
        target[0],
    )
    recon_error = error.astype(F32)[None]
    pre_grad = jnp.where(pre_acts > 0, grad[None], 0.0)
    return recon_error, pre_grad


def solution(mesh):
    return jax.shard_map(
        functools.partial(on_device, mesh.shape["layer"], mesh.shape["feat"]),
        mesh=mesh,
        in_specs=(
            P("layer", None, "feat"),
            P("layer", None, "feat", None),
            P("layer", "feat"),
            P("layer", None, "feat"),
        ),
        out_specs=(P("layer", None, "feat"), P("layer", None, "feat")),
        check_vma=False,
    )
```

```python
import functools

import jax
import jax.numpy as jnp
from jax import lax
from jax.experimental import pallas as pl
from jax.experimental.pallas import tpu as pltpu
from jax.sharding import PartitionSpec as P

MESH = pl.DeviceIdType.MESH
F32 = jnp.float32
BF16 = jnp.bfloat16


def kernel(
    n_layer, n_feat, n_step, n_block, lag_half, lag_mid, lag_outer,
    pre_ref, dec_ref, bias_ref, tgt_ref,
    err_ref, grad_ref,
    acts, weights, own, arrived, sent, half_in, error, terms, terms_in, tgt, pre, bias,
    w_sem, t_sem, pre_sem, bias_sem, out_sem,
    act_send, act_recv, p_send, p_recv, h_send, h_recv,
    e_in_send, e_out_send, e_recv, f_send, f_recv, term_send, term_recv,
):
    layer, feat = lax.axis_index("layer"), lax.axis_index("feat")
    tokens, width = pre.shape
    model = weights.shape[1]
    shard = tgt.shape[1]
    half = model // 2
    rows_step, rows_block = tokens // n_step, tokens // n_block
    per_block = n_step // n_block
    tile = 512 if model % 512 == 0 else model
    mid = n_feat // 2
    left = feat < mid
    inward = jnp.where(left, feat + 1, feat - 1)
    outward = jnp.where(left, feat - 1, feat + 1)
    has_outward = jnp.logical_and(feat > 0, feat < n_feat - 1)
    is_mid = jnp.logical_or(feat == mid - 1, feat == mid)
    not_mid = jnp.logical_not(is_mid)

    def layer_cols(index):
        return pl.ds(pl.multiple_of(index * width, width), width)

    near = pl.ds(pl.multiple_of(jnp.where(left, 0, half), half), half)
    far = pl.ds(pl.multiple_of(jnp.where(left, half, 0), half), half)
    own_cols = pl.ds(pl.multiple_of(feat * shard, shard), shard)

    def step_rows(i):
        return pl.ds(pl.multiple_of(i * rows_step, rows_step), rows_step)

    def block_rows(b):
        return pl.ds(pl.multiple_of(b * rows_block, rows_block), rows_block)

    pre_copy = pltpu.make_async_copy(pre_ref, pre, pre_sem)
    pre_copy.start()
    bias_copy = pltpu.make_async_copy(bias_ref, bias, bias_sem)
    bias_copy.start()

    def w_copy(s):
        rows = pl.ds(s * width, width)
        return pltpu.make_async_copy(dec_ref.at[rows, :], weights.at[rows, :], w_sem.at[s])

    for s in range(n_layer):
        w_copy(s).start()
    t_copy = pltpu.make_async_copy(tgt_ref, tgt, t_sem)
    t_copy.start()

    barrier = pltpu.get_barrier_semaphore()
    for t in range(n_layer):
        @pl.when(t != layer)
        def _():
            pl.semaphore_signal(barrier, inc=1, device_id=(t, feat), device_id_type=MESH)
    pl.semaphore_signal(barrier, inc=1, device_id=(layer, inward), device_id_type=MESH)

    @pl.when(has_outward)
    def _():
        pl.semaphore_signal(barrier, inc=1, device_id=(layer, outward), device_id_type=MESH)

    pre_copy.wait()
    acts[:, layer_cols(layer)] = jnp.maximum(pre[...], jnp.zeros((), BF16))
    for s in range(n_layer):
        @pl.when(s > layer)
        def _():
            acts[:, s * width:(s + 1) * width] = jnp.zeros((tokens, width), BF16)

    pl.semaphore_wait(barrier, n_layer + has_outward.astype(jnp.int32))

    def act_copy(t, b, s):
        rows = block_rows(b)
        view = acts.at[rows, layer_cols(s)]
        return pltpu.make_async_remote_copy(
            src_ref=view, dst_ref=view, send_sem=act_send.at[t, b], recv_sem=act_recv.at[s, b],
            device_id=(t, feat), device_id_type=MESH)

    def send_acts(b):
        for t in reversed(range(1, n_layer)):
            @pl.when(t > layer)
            def _():
                act_copy(t, b, layer).start()

    send_acts(0)


    def p_copy(i):
        rows = step_rows(i)
        return pltpu.make_async_remote_copy(
            src_ref=sent.at[rows, :], dst_ref=arrived.at[rows, :],
            send_sem=p_send.at[i], recv_sem=p_recv.at[i],
            device_id=(layer, inward), device_id_type=MESH)

    def h_copy(i):
        rows = step_rows(i)
        return pltpu.make_async_remote_copy(
            src_ref=sent.at[rows, far], dst_ref=half_in.at[rows, :],
            send_sem=h_send.at[i], recv_sem=h_recv.at[i],
            device_id=(layer, inward), device_id_type=MESH)

    def e_copy(i, cols, send, recv, to):
        rows = step_rows(i)
        view = error.at[rows, cols]
        return pltpu.make_async_remote_copy(
            src_ref=view, dst_ref=view, send_sem=send.at[i], recv_sem=recv.at[i],
            device_id=(layer, to), device_id_type=MESH)

    def out_copy(i):
        rows = step_rows(i)
        return pltpu.make_async_copy(error.at[rows, own_cols], err_ref.at[rows, :], out_sem.at[i])

    def forward(b):
        rows = block_rows(b)
        for s in range(n_layer - 1):
            @pl.when(s < layer)
            def _():
                act_copy(layer, b, s).wait_recv()

        def one(c, _):
            cols = pl.ds(pl.multiple_of(c * tile, tile), tile)
            own[rows, cols] = jnp.dot(acts[rows, :], weights[:, cols], preferred_element_type=F32)
            return 0

        lax.fori_loop(0, model // tile, one, 0)
        own[rows, own_cols] += bias[...].astype(F32) - tgt[rows, :].astype(F32)

    def send_partial(i):
        rows = step_rows(i)

        @pl.when(has_outward)
        def _():
            p_copy(i).wait_recv()

            @pl.when(is_mid)
            def _():
                sent[rows, far] = (own[rows, far] + arrived[rows, far].astype(F32)).astype(BF16)
                h_copy(i).start()
                own[rows, near] += arrived[rows, near].astype(F32)

            @pl.when(not_mid)
            def _():
                sent[rows, :] = (own[rows, :] + arrived[rows, :].astype(F32)).astype(BF16)
                p_copy(i).start()

        @pl.when(jnp.logical_not(has_outward))
        def _():
            @pl.when(is_mid)
            def _():
                sent[rows, far] = own[rows, far].astype(BF16)
                h_copy(i).start()

            @pl.when(not_mid)
            def _():
                sent[rows, :] = own[rows, :].astype(BF16)
                p_copy(i).start()

    def finish_half(i):
        rows = step_rows(i)
        h_copy(i).wait_recv()
        error[rows, near] = (own[rows, near] + half_in[rows, :].astype(F32)).astype(BF16)
        e_copy(i, near, e_in_send, f_recv, inward).start()

        @pl.when(has_outward)
        def _():
            e_copy(i, near, e_out_send, e_recv, outward).start()

    def pass_error(i):
        @pl.when(not_mid)
        def _():
            e_copy(i, near, e_out_send, e_recv, inward).wait_recv()

            @pl.when(has_outward)
            def _():
                e_copy(i, near, e_out_send, e_recv, outward).start()

        e_copy(i, far, f_send, f_recv, inward).wait_recv()

        @pl.when(has_outward)
        def _():
            e_copy(i, far, f_send, f_recv, outward).start()

        out_copy(i).start()

    def term_copy(s, b, t):
        rows = block_rows(b)
        return pltpu.make_async_remote_copy(
            src_ref=terms.at[rows, layer_cols(s)], dst_ref=terms_in.at[t, rows, :],
            send_sem=term_send.at[s, b], recv_sem=term_recv.at[t, b],
            device_id=(s, feat), device_id_type=MESH)

    def backward(b):
        rows = block_rows(b)
        step = 2 * width

        def one(c, _):
            cols = pl.ds(pl.multiple_of(c * step, step), step)
            terms[rows, cols] = lax.dot_general(
                error[rows, :], weights[cols, :], (((1,), (1,)), ((), ())),
                preferred_element_type=F32).astype(BF16)
            return 0

        lax.fori_loop(0, n_layer // 2, one, 0)
        for s in range(n_layer - 1):
            @pl.when(s < layer)
            def _():
                term_copy(s, b, layer).start()

    def collect(b):
        rows = block_rows(b)
        grad_ref[rows, :] = terms[rows, layer_cols(layer)].astype(F32)
        for t in range(1, n_layer):
            @pl.when(t > layer)
            def _():
                term_copy(layer, b, t).wait_recv()
                grad_ref[rows, :] += terms_in[t, rows, :].astype(F32)

    lag = jnp.where(is_mid, lag_mid, lag_outer)

    for s in range(n_layer):
        w_copy(s).wait()
    t_copy.wait()
    bias_copy.wait()
    forward(0)
    if n_block > 1:
        send_acts(1)

    def body(i, _):
        h = i - lag_half

        @pl.when(i < n_step)
        def _():
            send_partial(i)

        @pl.when(jnp.logical_and(is_mid, jnp.logical_and(h >= 0, h < n_step)))
        def _():
            finish_half(h)

        j = i - lag

        @pl.when(jnp.logical_and(j >= 0, j < n_step))
        def _():
            pass_error(j)

        @pl.when(jnp.logical_and(j >= 0, jnp.logical_and(j < n_step, lax.rem(j, per_block) == per_block - 1)))
        def _():
            b = lax.div(j, per_block)
            backward(b)

            @pl.when(b >= 2)
            def _():
                collect(b - 2)

        nxt = lax.div(i + 1, per_block)

        @pl.when(jnp.logical_and(nxt < n_block, lax.rem(i + 1, per_block) == 0))
        def _():
            forward(nxt)

            @pl.when(nxt + 1 < n_block)
            def _():
                send_acts(nxt + 1)

        return 0

    lax.fori_loop(0, n_step + max(lag_mid, lag_outer), body, 0)

    def tail(b, _):
        collect(b)
        return 0

    lax.fori_loop(max(n_block - 2, 0), n_block, tail, 0)

    def drain(i, _):
        @pl.when(not_mid)
        def _():
            p_copy(i).wait_send()

        @pl.when(is_mid)
        def _():
            h_copy(i).wait_send()
            e_copy(i, near, e_in_send, f_recv, inward).wait_send()

        @pl.when(has_outward)
        def _():
            e_copy(i, near, e_out_send, e_recv, outward).wait_send()
            e_copy(i, far, f_send, f_recv, outward).wait_send()

        out_copy(i).wait()
        return 0

    lax.fori_loop(0, n_step, drain, 0)

    def drain_block(b, _):
        for t in range(1, n_layer):
            @pl.when(t > layer)
            def _():
                act_copy(t, b, layer).wait_send()
        for s in range(n_layer - 1):
            @pl.when(s < layer)
            def _():
                term_copy(s, b, layer).wait_send()
        return 0

    lax.fori_loop(0, n_block, drain_block, 0)


def on_device(n_layer, n_feat, pre_acts, decoder, dec_bias, target):
    _, tokens, width = pre_acts.shape
    model = decoder.shape[3]
    shard = target.shape[2]
    n_step, n_block = 16, 8
    any_space = pl.BlockSpec(memory_space=pl.ANY)
    vmem = pl.BlockSpec(memory_space=pltpu.VMEM)
    dma = pltpu.SemaphoreType.DMA
    flops = 4 * tokens * n_layer * width * model
    error, grad = pl.pallas_call(
        functools.partial(kernel, n_layer, n_feat, n_step, n_block, 1, 3, 8),
        out_shape=(
            jax.ShapeDtypeStruct((tokens, shard), BF16),
            jax.ShapeDtypeStruct((tokens, width), F32),
        ),
        in_specs=[any_space] * 4,
        out_specs=(any_space, vmem),
        scratch_shapes=[
            pltpu.VMEM((tokens, n_layer * width), BF16),
            pltpu.VMEM((n_layer * width, model), BF16),
            pltpu.VMEM((tokens, model), F32),
            pltpu.VMEM((tokens, model), BF16),
            pltpu.VMEM((tokens, model), BF16),
            pltpu.VMEM((tokens, model // 2), BF16),
            pltpu.VMEM((tokens, model), BF16),
            pltpu.VMEM((tokens, n_layer * width), BF16),
            pltpu.VMEM((n_layer, tokens, width), BF16),
            pltpu.VMEM((tokens, shard), BF16),
            pltpu.VMEM((tokens, width), BF16),
            pltpu.VMEM((1, shard), BF16),
            dma((n_layer,)), dma, dma, dma, dma((n_step,)),
            dma((n_layer, n_block)), dma((n_layer, n_block)),
            dma((n_step,)), dma((n_step,)), dma((n_step,)), dma((n_step,)),
            dma((n_step,)), dma((n_step,)), dma((n_step,)), dma((n_step,)), dma((n_step,)),
            dma((n_layer, n_block)), dma((n_layer, n_block)),
        ],
        compiler_params=pltpu.CompilerParams(
            collective_id=0, has_side_effects=True, vmem_limit_bytes=62 * 1024 * 1024),
        cost_estimate=pl.CostEstimate(
            flops=flops, bytes_accessed=2 * n_layer * width * model, transcendentals=0),
    )(
        pre_acts[0],
        decoder.reshape(n_layer * width, model),
        dec_bias,
        target[0],
    )
    recon_error = error.astype(F32)[None]
    pre_grad = jnp.where(pre_acts > 0, grad[None], 0.0)
    return recon_error, pre_grad


def solution(mesh):
    return jax.shard_map(
        functools.partial(on_device, mesh.shape["layer"], mesh.shape["feat"]),
        mesh=mesh,
        in_specs=(
            P("layer", None, "feat"),
            P("layer", None, "feat", None),
            P("layer", "feat"),
            P("layer", None, "feat"),
        ),
        out_specs=(P("layer", None, "feat"), P("layer", None, "feat")),
        check_vma=False,
    )
```

```python
import functools

import jax
import jax.numpy as jnp
from jax import lax
from jax.experimental import pallas as pl
from jax.experimental.pallas import tpu as pltpu
from jax.sharding import PartitionSpec as P

MESH = pl.DeviceIdType.MESH
F32 = jnp.float32
BF16 = jnp.bfloat16


def kernel(
    n_layer, n_feat, n_step, n_block, lag_half, lag_mid, lag_outer,
    pre_ref, dec_ref, bias_ref, tgt_ref,
    err_ref, grad_ref,
    acts, weights, own, arrived, sent, half_in, error, terms, terms_in, tgt, pre, bias,
    w_sem, t_sem, pre_sem, bias_sem, out_sem,
    act_send, act_recv, p_send, p_recv, h_send, h_recv,
    e_in_send, e_out_send, e_recv, f_send, f_recv, term_send, term_recv,
):
    layer, feat = lax.axis_index("layer"), lax.axis_index("feat")
    tokens, width = pre.shape
    model = weights.shape[1]
    shard = tgt.shape[1]
    half = model // 2
    rows_step, rows_block = tokens // n_step, tokens // n_block
    per_block = n_step // n_block
    tile = model // 2
    mid = n_feat // 2
    left = feat < mid
    inward = jnp.where(left, feat + 1, feat - 1)
    outward = jnp.where(left, feat - 1, feat + 1)
    has_outward = jnp.logical_and(feat > 0, feat < n_feat - 1)
    is_mid = jnp.logical_or(feat == mid - 1, feat == mid)
    not_mid = jnp.logical_not(is_mid)

    def layer_cols(index):
        return pl.ds(pl.multiple_of(index * width, width), width)

    near = pl.ds(pl.multiple_of(jnp.where(left, 0, half), half), half)
    far = pl.ds(pl.multiple_of(jnp.where(left, half, 0), half), half)
    own_cols = pl.ds(pl.multiple_of(feat * shard, shard), shard)

    def step_rows(i):
        return pl.ds(pl.multiple_of(i * rows_step, rows_step), rows_step)

    def block_rows(b):
        return pl.ds(pl.multiple_of(b * rows_block, rows_block), rows_block)

    pre_copy = pltpu.make_async_copy(pre_ref, pre, pre_sem)
    pre_copy.start()
    bias_copy = pltpu.make_async_copy(bias_ref, bias, bias_sem)
    bias_copy.start()

    def w_copy(s):
        rows = pl.ds(s * width, width)
        return pltpu.make_async_copy(dec_ref.at[rows, :], weights.at[rows, :], w_sem.at[s])

    for s in range(n_layer):
        w_copy(s).start()
    t_copy = pltpu.make_async_copy(tgt_ref, tgt, t_sem)
    t_copy.start()

    barrier = pltpu.get_barrier_semaphore()
    for t in range(n_layer):
        @pl.when(t != layer)
        def _():
            pl.semaphore_signal(barrier, inc=1, device_id=(t, feat), device_id_type=MESH)
    pl.semaphore_signal(barrier, inc=1, device_id=(layer, inward), device_id_type=MESH)

    @pl.when(has_outward)
    def _():
        pl.semaphore_signal(barrier, inc=1, device_id=(layer, outward), device_id_type=MESH)

    pre_copy.wait()
    acts[:, layer_cols(layer)] = jnp.maximum(pre[...], jnp.zeros((), BF16))
    for s in range(n_layer):
        @pl.when(s > layer)
        def _():
            acts[:, s * width:(s + 1) * width] = jnp.zeros((tokens, width), BF16)

    pl.semaphore_wait(barrier, n_layer + has_outward.astype(jnp.int32))

    def act_copy(t, b, s):
        rows = block_rows(b)
        view = acts.at[rows, layer_cols(s)]
        return pltpu.make_async_remote_copy(
            src_ref=view, dst_ref=view, send_sem=act_send.at[t, b], recv_sem=act_recv.at[s, b],
            device_id=(t, feat), device_id_type=MESH)

    def send_acts(b):
        for t in reversed(range(1, n_layer)):
            @pl.when(t > layer)
            def _():
                act_copy(t, b, layer).start()

    send_acts(0)


    def p_copy(i):
        rows = step_rows(i)
        return pltpu.make_async_remote_copy(
            src_ref=sent.at[rows, :], dst_ref=arrived.at[rows, :],
            send_sem=p_send.at[i], recv_sem=p_recv.at[i],
            device_id=(layer, inward), device_id_type=MESH)

    def h_copy(i):
        rows = step_rows(i)
        return pltpu.make_async_remote_copy(
            src_ref=sent.at[rows, far], dst_ref=half_in.at[rows, :],
            send_sem=h_send.at[i], recv_sem=h_recv.at[i],
            device_id=(layer, inward), device_id_type=MESH)

    def e_copy(i, cols, send, recv, to):
        rows = step_rows(i)
        view = error.at[rows, cols]
        return pltpu.make_async_remote_copy(
            src_ref=view, dst_ref=view, send_sem=send.at[i], recv_sem=recv.at[i],
            device_id=(layer, to), device_id_type=MESH)

    def out_copy(i):
        rows = step_rows(i)
        return pltpu.make_async_copy(error.at[rows, own_cols], err_ref.at[rows, :], out_sem.at[i])

    def forward(b):
        rows = block_rows(b)
        for s in range(n_layer - 1):
            @pl.when(s < layer)
            def _():
                act_copy(layer, b, s).wait_recv()

        def one(c, _):
            cols = pl.ds(pl.multiple_of(c * tile, tile), tile)
            own[rows, cols] = jnp.dot(acts[rows, :], weights[:, cols], preferred_element_type=F32)
            return 0

        lax.fori_loop(0, model // tile, one, 0)
        own[rows, own_cols] += bias[...].astype(F32) - tgt[rows, :].astype(F32)

    def send_partial(i):
        rows = step_rows(i)

        @pl.when(has_outward)
        def _():
            p_copy(i).wait_recv()

            @pl.when(is_mid)
            def _():
                sent[rows, far] = (own[rows, far] + arrived[rows, far].astype(F32)).astype(BF16)
                h_copy(i).start()
                own[rows, near] += arrived[rows, near].astype(F32)

            @pl.when(not_mid)
            def _():
                sent[rows, :] = (own[rows, :] + arrived[rows, :].astype(F32)).astype(BF16)
                p_copy(i).start()

        @pl.when(jnp.logical_not(has_outward))
        def _():
            @pl.when(is_mid)
            def _():
                sent[rows, far] = own[rows, far].astype(BF16)
                h_copy(i).start()

            @pl.when(not_mid)
            def _():
                sent[rows, :] = own[rows, :].astype(BF16)
                p_copy(i).start()

    def finish_half(i):
        rows = step_rows(i)
        h_copy(i).wait_recv()
        error[rows, near] = (own[rows, near] + half_in[rows, :].astype(F32)).astype(BF16)
        e_copy(i, near, e_in_send, f_recv, inward).start()

        @pl.when(has_outward)
        def _():
            e_copy(i, near, e_out_send, e_recv, outward).start()

    def pass_error(i):
        @pl.when(not_mid)
        def _():
            e_copy(i, near, e_out_send, e_recv, inward).wait_recv()

            @pl.when(has_outward)
            def _():
                e_copy(i, near, e_out_send, e_recv, outward).start()

        e_copy(i, far, f_send, f_recv, inward).wait_recv()

        @pl.when(has_outward)
        def _():
            e_copy(i, far, f_send, f_recv, outward).start()

        out_copy(i).start()

    def term_copy(s, b, t):
        rows = block_rows(b)
        return pltpu.make_async_remote_copy(
            src_ref=terms.at[rows, layer_cols(s)], dst_ref=terms_in.at[t, rows, :],
            send_sem=term_send.at[s, b], recv_sem=term_recv.at[t, b],
            device_id=(s, feat), device_id_type=MESH)

    def backward(b):
        rows = block_rows(b)
        group = 4 if n_layer % 4 == 0 else 1
        step = group * width

        def one(c, _):
            cols = pl.ds(pl.multiple_of(c * step, step), step)
            terms[rows, cols] = lax.dot_general(
                error[rows, :], weights[cols, :], (((1,), (1,)), ((), ())),
                preferred_element_type=F32).astype(BF16)
            return 0

        lax.fori_loop(0, n_layer // group, one, 0)
        for s in range(n_layer - 1):
            @pl.when(s < layer)
            def _():
                term_copy(s, b, layer).start()

    def collect(b):
        rows = block_rows(b)
        grad_ref[rows, :] = terms[rows, layer_cols(layer)].astype(F32)
        for t in range(1, n_layer):
            @pl.when(t > layer)
            def _():
                term_copy(layer, b, t).wait_recv()
                grad_ref[rows, :] += terms_in[t, rows, :].astype(F32)

    lag = jnp.where(is_mid, lag_mid, lag_outer)

    for s in range(n_layer):
        w_copy(s).wait()
    t_copy.wait()
    bias_copy.wait()
    forward(0)
    if n_block > 1:
        send_acts(1)

    def body(i, _):
        h = i - lag_half

        @pl.when(i < n_step)
        def _():
            send_partial(i)

        @pl.when(jnp.logical_and(is_mid, jnp.logical_and(h >= 0, h < n_step)))
        def _():
            finish_half(h)

        j = i - lag

        @pl.when(jnp.logical_and(j >= 0, j < n_step))
        def _():
            pass_error(j)

        @pl.when(jnp.logical_and(j >= 0, jnp.logical_and(j < n_step, lax.rem(j, per_block) == per_block - 1)))
        def _():
            b = lax.div(j, per_block)
            backward(b)

            @pl.when(b >= 2)
            def _():
                collect(b - 2)

        nxt = lax.div(i + 1, per_block)

        @pl.when(jnp.logical_and(nxt < n_block, lax.rem(i + 1, per_block) == 0))
        def _():
            forward(nxt)

            @pl.when(nxt + 1 < n_block)
            def _():
                send_acts(nxt + 1)

        return 0

    lax.fori_loop(0, n_step + max(lag_mid, lag_outer), body, 0)

    def tail(b, _):
        collect(b)
        return 0

    lax.fori_loop(max(n_block - 2, 0), n_block, tail, 0)

    def drain(i, _):
        @pl.when(not_mid)
        def _():
            p_copy(i).wait_send()

        @pl.when(is_mid)
        def _():
            h_copy(i).wait_send()
            e_copy(i, near, e_in_send, f_recv, inward).wait_send()

        @pl.when(has_outward)
        def _():
            e_copy(i, near, e_out_send, e_recv, outward).wait_send()
            e_copy(i, far, f_send, f_recv, outward).wait_send()

        out_copy(i).wait()
        return 0

    lax.fori_loop(0, n_step, drain, 0)

    def drain_block(b, _):
        for t in range(1, n_layer):
            @pl.when(t > layer)
            def _():
                act_copy(t, b, layer).wait_send()
        for s in range(n_layer - 1):
            @pl.when(s < layer)
            def _():
                term_copy(s, b, layer).wait_send()
        return 0

    lax.fori_loop(0, n_block, drain_block, 0)


def on_device(n_layer, n_feat, pre_acts, decoder, dec_bias, target):
    _, tokens, width = pre_acts.shape
    model = decoder.shape[3]
    shard = target.shape[2]
    n_step, n_block = 16, 8
    any_space = pl.BlockSpec(memory_space=pl.ANY)
    vmem = pl.BlockSpec(memory_space=pltpu.VMEM)
    dma = pltpu.SemaphoreType.DMA
    flops = 4 * tokens * n_layer * width * model
    error, grad = pl.pallas_call(
        functools.partial(kernel, n_layer, n_feat, n_step, n_block, 1, 3, 8),
        out_shape=(
            jax.ShapeDtypeStruct((tokens, shard), BF16),
            jax.ShapeDtypeStruct((tokens, width), F32),
        ),
        in_specs=[any_space] * 4,
        out_specs=(any_space, vmem),
        scratch_shapes=[
            pltpu.VMEM((tokens, n_layer * width), BF16),
            pltpu.VMEM((n_layer * width, model), BF16),
            pltpu.VMEM((tokens, model), F32),
            pltpu.VMEM((tokens, model), BF16),
            pltpu.VMEM((tokens, model), BF16),
            pltpu.VMEM((tokens, model // 2), BF16),
            pltpu.VMEM((tokens, model), BF16),
            pltpu.VMEM((tokens, n_layer * width), BF16),
            pltpu.VMEM((n_layer, tokens, width), BF16),
            pltpu.VMEM((tokens, shard), BF16),
            pltpu.VMEM((tokens, width), BF16),
            pltpu.VMEM((1, shard), BF16),
            dma((n_layer,)), dma, dma, dma, dma((n_step,)),
            dma((n_layer, n_block)), dma((n_layer, n_block)),
            dma((n_step,)), dma((n_step,)), dma((n_step,)), dma((n_step,)),
            dma((n_step,)), dma((n_step,)), dma((n_step,)), dma((n_step,)), dma((n_step,)),
            dma((n_layer, n_block)), dma((n_layer, n_block)),
        ],
        compiler_params=pltpu.CompilerParams(
            collective_id=0, has_side_effects=True, vmem_limit_bytes=62 * 1024 * 1024),
        cost_estimate=pl.CostEstimate(
            flops=flops, bytes_accessed=2 * n_layer * width * model, transcendentals=0),
    )(
        pre_acts[0],
        decoder.reshape(n_layer * width, model),
        dec_bias,
        target[0],
    )
    recon_error = error.astype(F32)[None]
    pre_grad = jnp.where(pre_acts > 0, grad[None], 0.0)
    return recon_error, pre_grad


def solution(mesh):
    return jax.shard_map(
        functools.partial(on_device, mesh.shape["layer"], mesh.shape["feat"]),
        mesh=mesh,
        in_specs=(
            P("layer", None, "feat"),
            P("layer", None, "feat", None),
            P("layer", "feat"),
            P("layer", None, "feat"),
        ),
        out_specs=(P("layer", None, "feat"), P("layer", None, "feat")),
        check_vma=False,
    )
```
